512 devices in a mesh: dp: 8 (over x, core), ctx: 64 (over z, y).
Axes of the slice: x: 4, y: 4, z: 16, core: 2. Of those that a mesh axis runs over, the one named last changes fastest.
Arguments:
- tokens: bfloat16 [8, 8192, 4096], P('dp', 'ctx'), may hold values from -8 to 8
- queries: bfloat16 [8, 8192, 4096], P('dp', 'ctx'), may hold values from -170 to 170
- key_weight: bfloat16 [4096, 512], P(('dp', 'ctx')), may hold values from -0.09375 to 0.09375
- value_weight: bfloat16 [4096, 512], P(('dp', 'ctx')), may hold values from -0.09375 to 0.09375
- bounds: int32 [3, 8, 8192], P(None, 'dp', 'ctx'), may hold values from 0 to 8191, as said below
Outputs:
- context: bfloat16 [8, 8192, 4096], P('dp', 'ctx')
The draws below stay inside these ranges and needn't reach their ends.
Inputs may be any that keep to these rules, and one draw needn't show every extreme that they name: Pairs are runs of consecutive tokens that cover each pack. For a token t, bounds[0] is the first position of its pair, bounds[1] the first of its chosen reply, bounds[2] the first of its rejected reply, the same for every token of the pair, with bounds[0] < bounds[1] < bounds[2] <= the pair's last position. A pair has at most 512 tokens, and every pack holds a pair of exactly 512.
All inputs are finite; a program needn't handle non-finite values.
Results may differ from the reference program's by a relative error of at most 0.011.
Values may be sent and summed in bfloat16 or wider, within the bound.
No kernel may reach another device: no remote copies, remote signals or barrier semaphores. Data moves between devices by JAX's collectives and lax.ppermute only.
A program may use at most 64 MiB of HBM per device.

```python
import math
import jax
import jax.numpy as jnp
from jax import lax

D = 4096
HEADS = 32
KVH = 4
HD = 128
TOK_DEV = 128
PACKS = 8
TOKENS = 8192
PAIR_MAX = 512


def draw_tokens(key, part):
    key = jax.random.fold_in(key, 11)
    shape = (PACKS, TOKENS, D)
    values = jnp.clip(jax.random.normal(key, shape, jnp.float32), -6.0, 6.0)
    return values.astype(jnp.bfloat16)


def draw_queries(key, part):
    key = jax.random.fold_in(key, 13)
    shape = (PACKS, TOKENS, HEADS * HD)
    values = jnp.clip(jax.random.normal(key, shape, jnp.float32), -6.0, 6.0)
    return values.astype(jnp.bfloat16)


def one_pack_bounds(key):
    block_count = TOKENS // PAIR_MAX
    shift_key, whole_key, cut_key, prompt_key, reply_key = jax.random.split(key, 5)
    shift = jax.random.randint(shift_key, (), 3, TOK_DEV)
    whole_block = jax.random.randint(whole_key, (), 0, block_count - 1)
    cuts = jax.random.randint(cut_key, (block_count - 1,), PAIR_MAX // 4, 3 * PAIR_MAX // 4 + 1)
    borders = shift + PAIR_MAX * jnp.arange(block_count, dtype=jnp.int32)
    inner = jnp.where(jnp.arange(block_count - 1) == whole_block, borders[:-1], borders[:-1] + cuts)
    starts = jnp.concatenate([jnp.zeros((1,), jnp.int32), borders, inner])
    places = jnp.arange(TOKENS, dtype=jnp.int32)
    below = starts[None, :] <= places[:, None]
    pair_begin = jnp.max(jnp.where(below, starts[None, :], 0), axis=1)
    pair_end = jnp.min(jnp.where(below, TOKENS, starts[None, :]), axis=1)
    length = pair_end - pair_begin
    prompt_table = jax.random.randint(prompt_key, (TOKENS,), 0, 1 << 20)
    reply_table = jax.random.randint(reply_key, (TOKENS,), 0, 1 << 20)
    prompt_len = 1 + prompt_table[pair_begin] % jnp.maximum(length // 2, 1)
    remainder = length - prompt_len
    chosen_len = 1 + reply_table[pair_begin] % jnp.maximum(remainder - 1, 1)
    chosen_at = pair_begin + prompt_len
    reject_at = chosen_at + chosen_len
    return jnp.stack([pair_begin, chosen_at, reject_at])


def draw_bounds(key, part):
    key = jax.random.fold_in(key, 17)
    pack_keys = jax.random.split(key, PACKS)
    layout = jax.vmap(one_pack_bounds)(pack_keys)
    return jnp.transpose(layout, (1, 0, 2)).astype(jnp.int32)


def shard_levels(rng, extent, cuts, low, top_value):
    def one(dim, parts):
        steps = jax.random.uniform(jax.random.fold_in(jax.random.fold_in(rng, 6), dim), (parts,), jnp.float32, low / len(cuts), top_value / len(cuts))
        return jnp.repeat(jnp.exp(steps), extent[dim] // parts).reshape((-1,) + (1,) * (len(extent) - dim - 1))

    factor_of = one(*cuts[0])
    for cut in cuts[1:]:
        factor_of = factor_of * one(*cut)
    return factor_of


def centred(stream_key, dims, scale, reach, cuts=(), held_as=jnp.bfloat16):
    level = shard_levels(stream_key, dims, cuts, -0.22, 0.18) if cuts else 1.0
    drawn = jax.random.normal(stream_key, dims, jnp.float32) * scale * level
    return jnp.minimum(jnp.maximum(drawn, -reach), reach).astype(held_as)


def setup_inputs(seed: int = 0) -> dict:
    key_of = jax.random.split(jax.random.key(seed), 6)
    tokens = draw_tokens(jax.random.fold_in(key_of[5], 71), 0)
    queries = draw_queries(jax.random.fold_in(key_of[5], 71), 0)
    key_weight = centred(key_of[2], (D, KVH * HD), D ** -0.5, 0.09375, ((0, 512),))
    value_weight = centred(key_of[3], (D, KVH * HD), D ** -0.5, 0.09375, ((0, 512),))
    bounds = draw_bounds(jax.random.fold_in(key_of[5], 71), 0)
    return {"tokens": tokens, "queries": queries, "key_weight": key_weight, "value_weight": value_weight, "bounds": bounds}


def frequencies(head_size):
    halves = jnp.arange(head_size // 2, dtype=jnp.float32)
    base_rate = 500000.0 ** (-2.0 * halves / head_size)
    wavelength = 2.0 * math.pi / base_rate
    mixing = (8192.0 / wavelength - 1.0) / 3.0
    middle = (1.0 - mixing) * base_rate / 8.0 + mixing * base_rate
    return jnp.where(wavelength < 2048.0, base_rate, jnp.where(wavelength > 8192.0, base_rate / 8.0, middle))


def positions(limits, places):
    return jnp.where(places < limits[2], places - limits[0], places - limits[0] - (limits[2] - limits[1]))


def rotate(vectors, offsets, rates):
    angles = offsets.astype(jnp.float32)[:, None] * rates[None, :]
    cos_part = jnp.cos(angles)[:, None, :]
    sin_part = jnp.sin(angles)[:, None, :]
    half_size = vectors.shape[-1] // 2
    lower_half = vectors[..., :half_size]
    upper_half = vectors[..., half_size:]
    return jnp.concatenate([lower_half * cos_part - upper_half * sin_part, upper_half * cos_part + lower_half * sin_part], axis=-1)


def reference(tokens, queries, key_weight, value_weight, bounds):
    rates = frequencies(HD)
    group_size = HEADS // KVH
    query_block = math.gcd(256, TOKENS)
    head_scale = HD ** -0.5

    def one_pack(inputs):
        activations, query_rows, limits = inputs
        places = jnp.arange(TOKENS, dtype=jnp.int32)
        offsets = positions(limits, places)
        key_rows = jnp.dot(activations, key_weight, preferred_element_type=jnp.float32).reshape(TOKENS, KVH, HD)
        key_rows = lax.optimization_barrier(rotate(key_rows, offsets, rates).astype(jnp.bfloat16))
        value_rows = jnp.dot(activations, value_weight, preferred_element_type=jnp.float32).astype(jnp.bfloat16)
        value_rows = lax.optimization_barrier(value_rows).reshape(TOKENS, KVH, HD)
        turned = rotate(query_rows.astype(jnp.float32).reshape(TOKENS, HEADS, HD), offsets, rates)
        turned = lax.optimization_barrier(turned.astype(jnp.bfloat16))
        padding = jnp.zeros((PAIR_MAX, KVH, HD), jnp.bfloat16)
        padded_keys = jnp.concatenate([padding, key_rows], axis=0)
        padded_values = jnp.concatenate([padding, value_rows], axis=0)

        def one_block(first_row):
            block_queries = lax.dynamic_slice_in_dim(turned, first_row, query_block, 0).astype(jnp.float32)
            block_queries = block_queries.reshape(query_block, KVH, group_size, HD)
            block_keys = lax.dynamic_slice_in_dim(padded_keys, first_row, query_block + PAIR_MAX, 0).astype(jnp.float32)
            block_values = lax.dynamic_slice_in_dim(padded_values, first_row, query_block + PAIR_MAX, 0).astype(jnp.float32)
            query_index = first_row + jnp.arange(query_block, dtype=jnp.int32)
            key_index = first_row - PAIR_MAX + jnp.arange(query_block + PAIR_MAX, dtype=jnp.int32)
            begin_at = lax.dynamic_slice_in_dim(limits[0], first_row, query_block, 0)
            chosen_at = lax.dynamic_slice_in_dim(limits[1], first_row, query_block, 0)
            reject_at = lax.dynamic_slice_in_dim(limits[2], first_row, query_block, 0)
            excluded = (query_index >= reject_at)[:, None] & (key_index[None, :] >= chosen_at[:, None]) & (key_index[None, :] < reject_at[:, None])
            visible = (key_index[None, :] >= begin_at[:, None]) & (key_index[None, :] <= query_index[:, None]) & jnp.logical_not(excluded)
            scores = jnp.einsum('qhgd,khd->hgqk', block_queries, block_keys) * head_scale
            highest = jnp.max(jnp.where(visible, scores, -jnp.inf), axis=-1, keepdims=True)
            weights = jnp.exp(jnp.where(visible, scores - highest, -jnp.inf))
            totals = jnp.sum(weights, axis=-1)
            rounded = lax.optimization_barrier(weights.astype(jnp.bfloat16)).astype(jnp.float32)
            context = jnp.einsum('hgqk,khd->qhgd', rounded, block_values)
            context = context / jnp.transpose(totals, (2, 0, 1))[..., None]
            return context.astype(jnp.bfloat16).reshape(query_block, HEADS * HD)

        block_starts = jnp.arange(0, TOKENS, query_block, dtype=jnp.int32)
        return lax.map(one_block, block_starts).reshape(TOKENS, HEADS * HD)

    return lax.map(one_pack, (tokens, queries, jnp.transpose(bounds, (1, 0, 2))))
```

```python
import functools
import math

import jax
import jax.numpy as jnp
from jax import lax
from jax.experimental import pallas as pl
from jax.experimental.pallas import tpu as pltpu
from jax.sharding import Mesh, PartitionSpec as P

HD = 128
NX, NC, NZ, NY = 4, 2, 16, 4
NEG_FILL = -1e30
BF16 = jnp.bfloat16
F32 = jnp.float32


def frequencies(head_size):
    halves = jnp.arange(head_size // 2, dtype=jnp.float32)
    base_rate = 500000.0 ** (-2.0 * halves / head_size)
    wavelength = 2.0 * math.pi / base_rate
    mixing = (8192.0 / wavelength - 1.0) / 3.0
    middle = (1.0 - mixing) * base_rate / 8.0 + mixing * base_rate
    return jnp.where(
        wavelength < 2048.0, base_rate, jnp.where(wavelength > 8192.0, base_rate / 8.0, middle)
    )


def positions(limits, places):
    return jnp.where(
        places < limits[2], places - limits[0], places - limits[0] - (limits[2] - limits[1])
    )


def cos_sin(offsets):
    angles = offsets[:, None] * frequencies(HD)[None, :]
    cos_part, sin_part = jnp.cos(angles), jnp.sin(angles)
    return (
        jnp.concatenate([cos_part, cos_part], axis=1),
        jnp.concatenate([-sin_part, sin_part], axis=1),
    )


def swap_halves(vectors):
    half = vectors.shape[-1] // 2
    return jnp.concatenate([vectors[..., half:], vectors[..., :half]], axis=-1)


def copies(block, count):
    return jnp.broadcast_to(block[None], (count,) + block.shape)


def project_kernel(core_ref, a_ref, b_ref, mine_ref, other_ref, cos_ref, sin_ref, out_ref, acc):
    step = pl.program_id(0)

    @pl.when(step == 0)
    def _():
        acc[...] = jnp.zeros_like(acc)

    acc[...] += jnp.dot(
        a_ref[...], mine_ref[0], preferred_element_type=F32
    ) + jnp.dot(b_ref[...], other_ref[0], preferred_element_type=F32)

    @pl.when(step == pl.num_programs(0) - 1)
    def _():
        keys = acc[:, :HD]
        out_ref[:, :HD] = (keys * cos_ref[...] + swap_halves(keys) * sin_ref[...]).astype(BF16)
        out_ref[:, HD:] = acc[:, HD:].astype(BF16)


def project(core, tokens, mine, other, cos, sin):
    rows = tokens.shape[0]
    depth = mine.shape[1]
    width = mine.shape[2]
    whole = lambda i, c: (0, 0)
    return pl.pallas_call(
        project_kernel,
        grid_spec=pltpu.PrefetchScalarGridSpec(
            num_scalar_prefetch=1,
            grid=(mine.shape[0],),
            in_specs=[
                pl.BlockSpec((rows, depth), lambda i, c: (0, 2 * i + c[0])),
                pl.BlockSpec((rows, depth), lambda i, c: (0, 2 * i + 1 - c[0])),
                pl.BlockSpec((1, depth, width), lambda i, c: (i, 0, 0)),
                pl.BlockSpec((1, depth, width), lambda i, c: (i, 0, 0)),
                pl.BlockSpec((rows, HD), whole),
                pl.BlockSpec((rows, HD), whole),
            ],
            out_specs=pl.BlockSpec((rows, width), whole),
            scratch_shapes=[pltpu.VMEM((rows, width), F32)],
        ),
        out_shape=jax.ShapeDtypeStruct((rows, width), BF16),
        compiler_params=pltpu.CompilerParams(vmem_limit_bytes=24 * 1024 * 1024),
        name="project",
    )(core, tokens, tokens, mine, other, cos, sin)


def attend_kernel(group, scale, q_ref, kv_ref, bias_ref, out_ref):
    keys = kv_ref[0, :, :HD]
    values = kv_ref[0, :, HD:]
    for head in range(group):
        cols = slice(head * HD, (head + 1) * HD)
        scores = lax.dot_general(
            q_ref[:, cols], keys, (((1,), (1,)), ((), ())), preferred_element_type=F32
        )
        scores = scores + bias_ref[...]
        highest = jnp.max(scores, axis=-1, keepdims=True)
        weights = jnp.exp2((scores - highest) * scale)
        totals = jnp.sum(weights, axis=-1, keepdims=True)
        context = jnp.dot(weights.astype(BF16), values, preferred_element_type=F32)
        out_ref[:, cols] = (context / totals).astype(BF16)


def attend(turned, window, bias):
    rows, width = turned.shape
    kv_heads, span, _ = window.shape
    per = width // kv_heads
    scale = HD ** (-0.5) * math.log2(math.e)
    return pl.pallas_call(
        functools.partial(attend_kernel, per // HD, scale),
        grid=(kv_heads,),
        in_specs=[
            pl.BlockSpec((rows, per), lambda g: (0, g)),
            pl.BlockSpec((1, span, 2 * HD), lambda g: (g, 0, 0)),
            pl.BlockSpec((rows, span), lambda g: (0, 0)),
        ],
        out_specs=pl.BlockSpec((rows, per), lambda g: (0, g)),
        out_shape=jax.ShapeDtypeStruct((rows, width), BF16),
        compiler_params=pltpu.CompilerParams(vmem_limit_bytes=24 * 1024 * 1024),
        name="attend",
    )(turned, window, bias)


def shards(tokens, queries, key_weight, value_weight, bounds):
    local_len = tokens.shape[1]
    features = tokens.shape[2]
    kv_heads = key_weight.shape[1] // HD
    rows = key_weight.shape[0]
    slab = NY * local_len
    y_at = lax.axis_index("y")
    core = lax.axis_index("core").astype(jnp.int32)
    my_index = lax.axis_index("z") * NY + y_at

    gathered = lax.all_to_all(copies(tokens[0], NY), "y", 0, 0).reshape(slab, features)

    places = my_index * local_len + jnp.arange(local_len, dtype=jnp.int32)
    limits = bounds[:, 0, :]
    offsets = positions(limits, places)

    by_head = jnp.concatenate(
        [
            key_weight.reshape(rows, kv_heads, HD),
            value_weight.reshape(rows, kv_heads, HD),
        ],
        axis=-1,
    ).transpose(1, 0, 2)
    coded = jnp.concatenate([offsets // 256, offsets % 256]).astype(BF16)
    parcel = jnp.concatenate(
        [by_head, jnp.broadcast_to(coded[None, None], (kv_heads, 8, 2 * HD))], axis=1
    )
    parcel = lax.all_to_all(parcel, "y", 0, 0)
    slab_code = parcel[:, rows, :].astype(F32)
    slab_offsets = (slab_code[:, :local_len] * 256.0 + slab_code[:, local_len:]).reshape(slab)
    weight = parcel[:, :rows, :].reshape(NY * rows, 2 * HD)
    weight = lax.all_to_all(copies(weight, NZ), "z", 0, 0).reshape(NZ * NY * rows, 2 * HD)
    weight = lax.all_to_all(copies(weight, NX), "x", 0, 0)
    other = lax.ppermute(weight, "core", [(0, 1), (1, 0)])

    cos, sin = cos_sin(slab_offsets)
    own_slab = project(core[None], gathered, weight, other, cos, sin)
    last_slab = lax.ppermute(own_slab, "z", [(i, i + 1) for i in range(NZ - 1)])
    span = slab + local_len
    both = jnp.concatenate([last_slab, own_slab], axis=0)
    windows = jnp.stack([both[i * local_len : i * local_len + span] for i in range(NY)])
    window = lax.all_to_all(windows, "y", 0, 0)

    own_cos, own_sin = cos_sin(offsets.astype(F32))
    raw = queries[0].astype(F32).reshape(local_len, -1, HD)
    turned = (raw * own_cos[:, None, :] + swap_halves(raw) * own_sin[:, None, :]).astype(BF16)
    turned = turned.reshape(local_len, -1)

    key_index = my_index * local_len - slab + jnp.arange(span, dtype=jnp.int32)
    begin_at, chosen_at, reject_at = (limits[i][:, None] for i in range(3))
    place = places[:, None]
    excluded = (place >= reject_at) & (key_index >= chosen_at) & (key_index < reject_at)
    visible = (key_index >= begin_at) & (key_index <= place) & jnp.logical_not(excluded)
    bias = jnp.where(visible, 0.0, NEG_FILL).astype(F32)

    return attend(turned, window, bias)[None]


def solution(mesh):
    fine = Mesh(mesh.devices.reshape(NX, NC, NZ, NY), ("x", "core", "z", "y"))
    dp, ctx = ("x", "core"), ("z", "y")
    return jax.shard_map(
        shards,
        mesh=fine,
        in_specs=(
            P(dp, ctx, None),
            P(dp, ctx, None),
            P(dp + ctx, None),
            P(dp + ctx, None),
            P(None, dp, ctx),
        ),
        out_specs=P(dp, ctx, None),
        check_vma=False,
    )
```

```python
import functools
import math

import jax
import jax.numpy as jnp
from jax import lax
from jax.experimental import pallas as pl
from jax.experimental.pallas import tpu as pltpu
from jax.sharding import Mesh, PartitionSpec as P

HD = 128
NX, NC, NZ, NY = 4, 2, 16, 4
NEG_FILL = -1e30
BF16 = jnp.bfloat16
F32 = jnp.float32


def frequencies(head_size):
    halves = jnp.arange(head_size // 2, dtype=jnp.float32)
    base_rate = 500000.0 ** (-2.0 * halves / head_size)
    wavelength = 2.0 * math.pi / base_rate
    mixing = (8192.0 / wavelength - 1.0) / 3.0
    middle = (1.0 - mixing) * base_rate / 8.0 + mixing * base_rate
    return jnp.where(
        wavelength < 2048.0, base_rate, jnp.where(wavelength > 8192.0, base_rate / 8.0, middle)
    )


def positions(limits, places):
    return jnp.where(
        places < limits[2], places - limits[0], places - limits[0] - (limits[2] - limits[1])
    )


def cos_sin(offsets):
    angles = offsets[:, None] * frequencies(HD)[None, :]
    cos_part, sin_part = jnp.cos(angles), jnp.sin(angles)
    return (
        jnp.concatenate([cos_part, cos_part], axis=1),
        jnp.concatenate([-sin_part, sin_part], axis=1),
    )


def swap_halves(vectors):
    half = vectors.shape[-1] // 2
    return jnp.concatenate([vectors[..., half:], vectors[..., :half]], axis=-1)


def copies(block, count):
    return jnp.broadcast_to(block[None], (count,) + block.shape)


def project_kernel(core_ref, a_ref, b_ref, mine_ref, other_ref, cos_ref, sin_ref, out_ref, acc):
    step = pl.program_id(0)

    @pl.when(step == 0)
    def _():
        acc[...] = jnp.zeros_like(acc)

    acc[...] += jnp.dot(
        a_ref[...], mine_ref[0], preferred_element_type=F32
    ) + jnp.dot(b_ref[...], other_ref[0], preferred_element_type=F32)

    @pl.when(step == pl.num_programs(0) - 1)
    def _():
        keys = acc[:, :HD]
        out_ref[:, :HD] = (keys * cos_ref[...] + swap_halves(keys) * sin_ref[...]).astype(BF16)
        out_ref[:, HD:] = acc[:, HD:].astype(BF16)


def project(core, tokens, mine, other, cos, sin):
    rows = tokens.shape[0]
    depth = mine.shape[1]
    width = mine.shape[2]
    whole = lambda i, c: (0, 0)
    return pl.pallas_call(
        project_kernel,
        grid_spec=pltpu.PrefetchScalarGridSpec(
            num_scalar_prefetch=1,
            grid=(mine.shape[0],),
            in_specs=[
                pl.BlockSpec((rows, depth), lambda i, c: (0, 2 * i + c[0])),
                pl.BlockSpec((rows, depth), lambda i, c: (0, 2 * i + 1 - c[0])),
                pl.BlockSpec((1, depth, width), lambda i, c: (i, 0, 0)),
                pl.BlockSpec((1, depth, width), lambda i, c: (i, 0, 0)),
                pl.BlockSpec((rows, HD), whole),
                pl.BlockSpec((rows, HD), whole),
            ],
            out_specs=pl.BlockSpec((rows, width), whole),
            scratch_shapes=[pltpu.VMEM((rows, width), F32)],
        ),
        out_shape=jax.ShapeDtypeStruct((rows, width), BF16),
        compiler_params=pltpu.CompilerParams(vmem_limit_bytes=24 * 1024 * 1024),
        name="project",
    )(core, tokens, tokens, mine, other, cos, sin)


def turn_kernel(group, q_ref, cos_ref, sin_ref, out_ref):
    rows = q_ref.shape[0]
    cos, sin = cos_ref[...], sin_ref[...]
    for head in range(group):
        raw = q_ref[:, head * HD : (head + 1) * HD].astype(F32)
        turned = raw * cos + swap_halves(raw) * sin
        out_ref[0, head * rows : (head + 1) * rows, :] = turned.astype(BF16)


def turn(queries, cos, sin, kv_heads):
    rows, width = queries.shape
    per = width // kv_heads
    stacked = rows * per // HD
    return pl.pallas_call(
        functools.partial(turn_kernel, per // HD),
        grid=(kv_heads,),
        in_specs=[
            pl.BlockSpec((rows, per), lambda g: (0, g)),
            pl.BlockSpec((rows, HD), lambda g: (0, 0)),
            pl.BlockSpec((rows, HD), lambda g: (0, 0)),
        ],
        out_specs=pl.BlockSpec((1, stacked, HD), lambda g: (g, 0, 0)),
        out_shape=jax.ShapeDtypeStruct((kv_heads, stacked, HD), BF16),
        compiler_params=pltpu.CompilerParams(vmem_limit_bytes=16 * 1024 * 1024),
        name="turn",
    )(queries, cos, sin)


def attend_kernel(part, scale, q_ref, kv_ref, bias_ref, out_ref, left, right, paired):
    rows = out_ref.shape[0]
    stacked = q_ref.shape[1]
    span = kv_ref.shape[1]

    @pl.when(pl.program_id(0) == 0)
    def _():
        row = lax.broadcasted_iota(jnp.int32, (rows, rows), 0)
        col = lax.broadcasted_iota(jnp.int32, (rows, rows), 1)
        left[:, HD:] = jnp.where(row == col, 1.0, 0.0).astype(BF16)
        right[HD:, :] = bias_ref[...]
        paired[:, HD:] = jnp.ones((span, HD), BF16)

    right[:HD, :] = kv_ref[0, :, :HD].T
    paired[:, :HD] = kv_ref[0, :, HD:]
    for first in range(0, stacked, part):
        heads = [
            jnp.concatenate([q_ref[0, at : at + rows, :], left[:, HD:]], axis=1)
            for at in range(first, first + part, rows)
        ]
        block = jnp.concatenate(heads, axis=0)
        scores = jnp.dot(block, right[...], preferred_element_type=F32)
        highest = jnp.max(scores, axis=-1, keepdims=True)
        weights = jnp.exp2((scores - highest) * scale).astype(BF16)
        sums = jnp.dot(weights, paired[...], preferred_element_type=F32)
        context = (sums[:, :HD] / sums[:, HD:]).astype(BF16)
        for at in range(0, part, rows):
            head = (first + at) // rows
            out_ref[:, head * HD : (head + 1) * HD] = context[at : at + rows, :]


def attend(turned, window, bias):
    kv_heads, stacked, _ = turned.shape
    rows, span = bias.shape
    per = stacked // rows * HD
    scale = HD ** (-0.5) * math.log2(math.e)
    return pl.pallas_call(
        functools.partial(attend_kernel, 2 * rows, scale),
        grid=(kv_heads,),
        in_specs=[
            pl.BlockSpec((1, stacked, HD), lambda g: (g, 0, 0)),
            pl.BlockSpec((1, span, 2 * HD), lambda g: (g, 0, 0)),
            pl.BlockSpec((rows, span), lambda g: (0, 0)),
        ],
        out_specs=pl.BlockSpec((rows, per), lambda g: (0, g)),
        out_shape=jax.ShapeDtypeStruct((rows, kv_heads * per), BF16),
        scratch_shapes=[
            pltpu.VMEM((rows, 2 * HD), BF16),
            pltpu.VMEM((2 * HD, span), BF16),
            pltpu.VMEM((span, 2 * HD), BF16),
        ],
        compiler_params=pltpu.CompilerParams(vmem_limit_bytes=24 * 1024 * 1024),
        name="attend",
    )(turned, window, bias)


def shards(tokens, queries, key_weight, value_weight, bounds):
    local_len = tokens.shape[1]
    kv_heads = key_weight.shape[1] // HD
    rows = key_weight.shape[0]
    slab = NY * local_len
    y_at = lax.axis_index("y")
    core = lax.axis_index("core").astype(jnp.int32)
    my_index = lax.axis_index("z") * NY + y_at

    gathered = lax.all_gather(tokens[0], "y", axis=0, tiled=True)

    places = my_index * local_len + jnp.arange(local_len, dtype=jnp.int32)
    limits = bounds[:, 0, :]
    offsets = positions(limits, places)

    by_head = jnp.concatenate(
        [
            key_weight.reshape(rows, kv_heads, HD),
            value_weight.reshape(rows, kv_heads, HD),
        ],
        axis=-1,
    ).transpose(1, 0, 2)
    coded = jnp.concatenate([offsets // 256, offsets % 256]).astype(BF16)
    parcel = jnp.concatenate(
        [by_head, jnp.broadcast_to(coded[None, None], (kv_heads, 8, 2 * HD))], axis=1
    )
    parcel = lax.all_to_all(parcel, "y", 0, 0)
    slab_code = parcel[:, rows, :].astype(F32)
    slab_offsets = (slab_code[:, :local_len] * 256.0 + slab_code[:, local_len:]).reshape(slab)
    weight = parcel[:, :rows, :].reshape(NY * rows, 2 * HD)
    weight = lax.all_to_all(copies(weight, NZ), "z", 0, 0).reshape(NZ * NY * rows, 2 * HD)
    weight = lax.all_to_all(copies(weight, NX), "x", 0, 0)
    other = lax.ppermute(weight, "core", [(0, 1), (1, 0)])

    cos, sin = cos_sin(slab_offsets)
    own_slab = project(core[None], gathered, weight, other, cos, sin)
    last_slab = lax.ppermute(own_slab, "z", [(i, i + 1) for i in range(NZ - 1)])
    span = slab + local_len
    both = jnp.concatenate([last_slab, own_slab], axis=0)
    windows = jnp.stack([both[i * local_len : i * local_len + span] for i in range(NY)])
    window = lax.all_to_all(windows, "y", 0, 0)

    own_cos, own_sin = cos_sin(offsets.astype(F32))
    turned = turn(queries[0], own_cos, own_sin, kv_heads)

    key_index = my_index * local_len - slab + jnp.arange(span, dtype=jnp.int32)
    begin_at, chosen_at, reject_at = (limits[i][:, None] for i in range(3))
    place = places[:, None]
    excluded = (place >= reject_at) & (key_index >= chosen_at) & (key_index < reject_at)
    visible = (key_index >= begin_at) & (key_index <= place) & jnp.logical_not(excluded)
    bias = jnp.where(visible, 0.0, NEG_FILL).astype(BF16)

    return attend(turned, window, bias)[None]


def solution(mesh):
    fine = Mesh(mesh.devices.reshape(NX, NC, NZ, NY), ("x", "core", "z", "y"))
    dp, ctx = ("x", "core"), ("z", "y")
    return jax.shard_map(
        shards,
        mesh=fine,
        in_specs=(
            P(dp, ctx, None),
            P(dp, ctx, None),
            P(dp + ctx, None),
            P(dp + ctx, None),
            P(None, dp, ctx),
        ),
        out_specs=P(dp, ctx, None),
        check_vma=False,
    )
```
